32 devices in a mesh: dp: 16 (over z, x, core), tensor: 2 (over y).
Axes of the slice: x: 2, y: 2, z: 4, core: 2. Of those that a mesh axis runs over, the one named last changes fastest.
Arguments:
- tokens: bfloat16 [1024, 16, 1024], P('tensor', 'dp'), may hold values from -6 to 6
- cond: bfloat16 [16, 1024], P('dp'), may hold values from -6 to 6
- qkv_weight: bfloat16 [1024, 3072], P('dp', 'tensor'), may hold values from -0.1875 to 0.1875
- out_weight: bfloat16 [1024, 1024], P('dp', 'tensor'), may hold values from -1.5 to 1.5
- up_weight: bfloat16 [1024, 4096], P('dp', 'tensor'), may hold values from -0.1875 to 0.1875
- down_weight: bfloat16 [1024, 4096], P('dp', 'tensor'), may hold values from -0.09375 to 0.09375
- ada_weight: bfloat16 [1024, 6144], P('dp'), may hold values from -0.1875 to 0.1875
- ada_bias: bfloat16 [6144], P('dp'), may hold values from -3 to 3
- cotangent: bfloat16 [1024, 16, 1024], P('tensor', 'dp'), may hold values from -6 to 6
Outputs:
- mixed: float32 [1024, 16, 1024], P('tensor', 'dp')
- grad_tokens: float32 [1024, 16, 1024], P('tensor', 'dp')
- grad_cond: float32 [16, 1024], P('dp')
- grad_qkv: float32 [1024, 3072], P('dp', 'tensor')
- grad_out: float32 [1024, 1024], P('dp', 'tensor')
- grad_up: float32 [1024, 4096], P('dp', 'tensor')
- grad_down: float32 [1024, 4096], P('dp', 'tensor')
- grad_ada: float32 [1024, 6144], P('dp')
- grad_ada_bias: float32 [6144], P('dp')
The draws below stay inside these ranges and needn't reach their ends.
All inputs are finite; a program needn't handle non-finite values.
Results may differ from the reference program's by a relative error of at most 0.02.
The reference program's roundings to bfloat16 on the way count: a program that leaves them out, or rounds other values in their place, can miss the bound.
Values may be sent and summed in bfloat16 or wider, within the bound.
A program may use at most 192 MiB of HBM per device.

```python
import jax
import jax.numpy as jnp
from jax import lax

D = 1024
HEADS = 16
HEAD_DIM = 64
FF = 4096
SEQ = 1024
LAT_DEV = 1
LAT = 16
N_TENSOR = 2


def level_of(own_key, dims, pieces, smallest, largest):
    factor_of, own = 1.0, jax.random.fold_in(own_key, 6)
    for dim, parts in pieces:
        steps = jnp.exp(jax.random.uniform(jax.random.fold_in(own, dim), (parts,), jnp.float32, smallest / len(pieces), largest / len(pieces)))
        factor_of = factor_of * jnp.repeat(steps, dims[dim] // parts).reshape([-1 if axis == dim else 1 for axis in range(len(dims))])
    return factor_of


def normal_values(stream_key, dims, spread, limit, cuts=(), dtype=jnp.bfloat16):
    level = level_of(stream_key, dims, cuts, -0.22, 0.18) if cuts else 1.0
    values = jax.random.normal(stream_key, dims, jnp.float32) * spread * level
    return jnp.minimum(jnp.maximum(values, -limit), limit).astype(dtype)


def setup_inputs(seed: int = 0) -> dict:
    key_of = jax.random.split(jax.random.key(seed), 10)
    tokens = normal_values(key_of[0], (SEQ, LAT, D), 1.0, 6.0, ((0, 2), (1, 16)))
    cond = normal_values(key_of[1], (LAT, D), 1.0, 6.0, ((0, 16),))
    qkv_weight = normal_values(key_of[2], (D, 3 * D), D ** -0.5, 0.1875, ((0, 16), (1, 2)))
    out_weight = normal_values(key_of[3], (D, D), (D // 64) ** -0.5, 1.5, ((0, 16), (1, 2)))
    up_weight = normal_values(key_of[4], (D, FF), D ** -0.5, 0.1875, ((0, 16), (1, 2)))
    down_weight = normal_values(key_of[5], (D, FF), FF ** -0.5, 0.09375, ((0, 16), (1, 2)))
    ada_weight = normal_values(key_of[6], (D, 6 * D), D ** -0.5, 0.1875, ((0, 16),))
    ada_bias = normal_values(key_of[7], (6 * D,), 0.5, 3.0, ((0, 16),))
    cotangent = normal_values(key_of[8], (SEQ, LAT, D), 1.0, 6.0, ((0, 2), (1, 16)))
    return {"tokens": tokens, "cond": cond, "qkv_weight": qkv_weight, "out_weight": out_weight, "up_weight": up_weight, "down_weight": down_weight, "ada_weight": ada_weight, "ada_bias": ada_bias, "cotangent": cotangent}


@jax.custom_vjp
def low(v):
    return lax.optimization_barrier(v.astype(jnp.bfloat16)).astype(jnp.float32)

@jax.custom_vjp
def low_back(v):
    return v

def low_keep(v):
    return (low(v), None)

def low_pass(kept, grad):
    return (grad,)

def back_keep(v):
    return (v, None)

def back_low(kept, grad):
    return (low(grad),)
low.defvjp(low_keep, low_pass)
low_back.defvjp(back_keep, back_low)
epsilon = 1e-06
highest = lax.Precision.HIGHEST

def layer_norm(inputs):
    centred = inputs - lax.optimization_barrier(jnp.mean(inputs, axis=-1, keepdims=True))
    return centred * lax.rsqrt(lax.optimization_barrier(jnp.mean(centred * centred, axis=-1, keepdims=True)) + epsilon)

def grouped(matrix):
    return matrix.reshape(matrix.shape[0], N_TENSOR, matrix.shape[1] // N_TENSOR)

def attend(qkv_heads):
    seq_len, latents = (qkv_heads.shape[0], qkv_heads.shape[1])
    queries = qkv_heads[:, :, :, 0]
    key_heads = qkv_heads[:, :, :, 1]
    value_heads = qkv_heads[:, :, :, 2]
    block_rows = min(512, seq_len)
    blocked = queries.reshape(seq_len // block_rows, block_rows, latents, HEADS, HEAD_DIM)
    score_scale = HEAD_DIM ** (-0.5)

    def one_block(query_block):
        scores = jnp.einsum('qghe,kghe->ghqk', query_block, key_heads, precision=highest) * score_scale
        weights = low(jax.nn.softmax(low_back(scores), axis=-1))
        return jnp.einsum('ghqk,kghe->qghe', weights, value_heads, precision=highest)
    results = lax.map(jax.checkpoint(one_block), blocked)
    return results.reshape(seq_len, latents, HEADS * HEAD_DIM)

def forward(group_tokens, group_cond, qkv_weight, out_weight, up_weight, down_weight, ada_weight, ada_bias):
    seq_len, latents = (group_tokens.shape[0], group_tokens.shape[1])
    cond_act = low(jax.nn.silu(group_cond))
    modulation = low_back(jnp.dot(cond_act, ada_weight, precision=highest, preferred_element_type=jnp.float32) + ada_bias)
    shift1, scale1, gate1, shift2, scale2, gate2 = jnp.split(modulation, 6, axis=-1)
    normed1 = low(layer_norm(group_tokens) * (1.0 + scale1) + shift1)
    spread1 = low_back(jnp.broadcast_to(normed1, (N_TENSOR,) + normed1.shape))
    query_key_value = jnp.einsum('tsgd,dte->sgte', spread1, grouped(qkv_weight), precision=highest).reshape(seq_len, latents, 3 * D)
    query_key_value = low(low_back(query_key_value))
    attended = low(low_back(attend(query_key_value.reshape(seq_len, latents, HEADS, 3, HEAD_DIM))))
    branch_terms = jnp.einsum('sgte,fte->tsgf', attended.reshape(seq_len, latents, N_TENSOR, D // N_TENSOR), grouped(out_weight), precision=highest)
    branch = low_back(lax.optimization_barrier(jnp.sum(low(branch_terms), axis=0)))
    middle = group_tokens + gate1 * branch
    normed2 = low(layer_norm(middle) * (1.0 + scale2) + shift2)
    spread2 = low_back(jnp.broadcast_to(normed2, (N_TENSOR,) + normed2.shape))
    hidden_activation = jnp.einsum('tsgd,dte->sgte', spread2, grouped(up_weight), precision=highest).reshape(seq_len, latents, FF)
    hidden_activation = low_back(hidden_activation)
    activation = low(jax.nn.gelu(hidden_activation, approximate=True))
    mlp_terms = jnp.einsum('sgte,fte->tsgf', activation.reshape(seq_len, latents, N_TENSOR, FF // N_TENSOR), grouped(down_weight), precision=highest)
    mlp_out = low_back(lax.optimization_barrier(jnp.sum(low(mlp_terms), axis=0)))
    return middle + gate2 * mlp_out

def reference(tokens, cond, qkv_weight, out_weight, up_weight, down_weight, ada_weight, ada_bias, cotangent):
    weights = tuple((matrix.astype(jnp.float32) for matrix in (qkv_weight, out_weight, up_weight, down_weight, ada_weight, ada_bias)))
    groups = LAT // LAT_DEV

    def by_group(array):
        return array.astype(jnp.float32).reshape(SEQ, groups, LAT_DEV, D).transpose(1, 0, 2, 3)
    inputs = (by_group(tokens), cond.astype(jnp.float32).reshape(groups, LAT_DEV, D), by_group(cotangent))

    def advance(totals, group):
        group_tokens, group_cond, group_cot = group
        result, pullback = jax.vjp(forward, group_tokens, group_cond, *weights)
        gradients = pullback(group_cot)
        totals = tuple((total + grad for total, grad in zip(totals, gradients[2:])))
        return (totals, (result, gradients[0], gradients[1]))
    zeros_init = tuple((jnp.zeros_like(matrix) for matrix in weights))
    totals, (mixed, grad_tokens, grad_cond) = lax.scan(advance, zeros_init, inputs)
    mixed = mixed.transpose(1, 0, 2, 3).reshape(SEQ, LAT, D)
    grad_tokens = grad_tokens.transpose(1, 0, 2, 3).reshape(SEQ, LAT, D)
    grad_cond = grad_cond.reshape(LAT, D)
    return (mixed, grad_tokens, grad_cond, totals[0], totals[1], totals[2], totals[3], totals[4], totals[5])
```

```python
import jax
import jax.numpy as jnp
from jax import lax
from jax.sharding import PartitionSpec as P

HEAD_DIM = 64


epsilon = 1e-06


def layer_norm(inputs):
    centred = inputs - jnp.mean(inputs, axis=-1, keepdims=True)
    return centred * lax.rsqrt(jnp.mean(centred * centred, axis=-1, keepdims=True) + epsilon)


def modulate(inputs, shift_vec, scale_vec):
    return layer_norm(inputs) * (1.0 + scale_vec) + shift_vec


def gelu_tanh(inputs):
    return jax.nn.gelu(inputs, approximate=True)


def split_heads(query_key_value):
    latents, seq_len, features = query_key_value.shape
    head_count = features // (3 * HEAD_DIM)
    divided = query_key_value.reshape(latents, seq_len, head_count, 3, HEAD_DIM).transpose(
        3, 0, 2, 1, 4
    )
    return (divided[0], divided[1], divided[2])


def attention_forward(query_key_value, score_scale):
    queries, key_heads, value_heads = split_heads(query_key_value)
    latents, head_count, seq_len, head_width = queries.shape
    block_rows = min(512, seq_len)
    num_blocks = seq_len // block_rows

    def per_latent(inputs):
        query_lat, key_lat, value_lat = inputs

        def per_block(query_block):
            scores = (
                jnp.einsum("hqe,hke->hqk", query_block, key_lat, preferred_element_type=jnp.float32)
                * score_scale
            )
            row_max = jnp.max(scores, axis=-1, keepdims=True)
            shifted = jnp.exp(scores - row_max)
            denom_sum = jnp.sum(shifted, axis=-1, keepdims=True)
            weights = (shifted / denom_sum).astype(jnp.bfloat16)
            result = jnp.einsum(
                "hqk,hke->hqe", weights, value_lat, preferred_element_type=jnp.float32
            )
            return (result, (row_max + jnp.log(denom_sum))[:, :, 0])

        query_blocks = query_lat.reshape(head_count, num_blocks, block_rows, head_width).transpose(
            1, 0, 2, 3
        )
        results, log_parts = lax.map(per_block, query_blocks)
        results = results.transpose(1, 0, 2, 3).reshape(head_count, seq_len, head_width)
        log_parts = log_parts.transpose(1, 0, 2).reshape(head_count, seq_len)
        return (results, log_parts)

    results, log_total = lax.map(per_latent, (queries, key_heads, value_heads))
    attended = (
        results.transpose(0, 2, 1, 3)
        .reshape(latents, seq_len, head_count * head_width)
        .astype(jnp.bfloat16)
    )
    return (attended, log_total)


def attention_backward(query_key_value, attended, log_total, grad_attended, score_scale):
    queries, key_heads, value_heads = split_heads(query_key_value)
    latents, head_count, seq_len, head_width = queries.shape
    grad_heads = grad_attended.reshape(latents, seq_len, head_count, head_width).transpose(
        0, 2, 1, 3
    )
    block_rows = min(512, seq_len)
    num_blocks = seq_len // block_rows

    def per_latent(inputs):
        query_lat, key_lat, value_lat, log_lat, grad_lat = inputs
        query_blocks = query_lat.reshape(head_count, num_blocks, block_rows, head_width).transpose(
            1, 0, 2, 3
        )
        grad_blocks = grad_lat.reshape(head_count, num_blocks, block_rows, head_width).transpose(
            1, 0, 2, 3
        )
        log_blocks = log_lat.reshape(head_count, num_blocks, block_rows).transpose(1, 0, 2)

        def advance(totals, pieces):
            grad_keys, grad_values = totals
            query_block, grad_block, log_block = pieces
            scores = (
                jnp.einsum("hqe,hke->hqk", query_block, key_lat, preferred_element_type=jnp.float32)
                * score_scale
            )
            probs = jnp.exp(scores - log_block[:, :, None])
            grad_probs = jnp.einsum(
                "hqe,hke->hqk", grad_block, value_lat, preferred_element_type=jnp.float32
            )
            delta = jnp.sum(grad_probs * probs, axis=-1, keepdims=True)
            grad_scores = (probs * (grad_probs - delta)).astype(jnp.bfloat16)
            grad_query = (
                jnp.einsum("hqk,hke->hqe", grad_scores, key_lat, preferred_element_type=jnp.float32)
                * score_scale
            )
            grad_keys = (
                grad_keys
                + jnp.einsum(
                    "hqk,hqe->hke", grad_scores, query_block, preferred_element_type=jnp.float32
                )
                * score_scale
            )
            grad_values = grad_values + jnp.einsum(
                "hqk,hqe->hke",
                probs.astype(jnp.bfloat16),
                grad_block,
                preferred_element_type=jnp.float32,
            )
            return ((grad_keys, grad_values), grad_query)

        zeros_init = jnp.zeros((head_count, seq_len, head_width), jnp.float32)
        (grad_keys, grad_values), grad_query = lax.scan(
            advance, (zeros_init, zeros_init), (query_blocks, grad_blocks, log_blocks)
        )
        grad_query = grad_query.transpose(1, 0, 2, 3).reshape(head_count, seq_len, head_width)
        return jnp.stack([grad_query, grad_keys, grad_values], 0)

    gradients = lax.map(per_latent, (queries, key_heads, value_heads, log_total, grad_heads))
    seq_first = gradients.transpose(0, 3, 2, 1, 4)
    return seq_first.reshape(latents, seq_len, head_count * 3 * head_width).astype(jnp.bfloat16)


def dp_partner(value, bit):
    size = lax.axis_size("dp")
    return lax.ppermute(value, "dp", [(index, index ^ bit) for index in range(size)])


def gather_small(value):
    size, me, bit = lax.axis_size("dp"), lax.axis_index("dp"), 1
    while bit < size:
        other = dp_partner(value, bit)
        upper = (me & bit) != 0
        value = jnp.concatenate([jnp.where(upper, other, value), jnp.where(upper, value, other)], axis=0)
        bit *= 2
    return value


def scatter_small(value):
    me, bit = lax.axis_index("dp"), lax.axis_size("dp") // 2
    while bit >= 1:
        half = value.shape[0] // 2
        upper = (me & bit) != 0
        low_half, high_half = value[:half], value[half:]
        kept = jnp.where(upper, high_half, low_half)
        value = kept + dp_partner(jnp.where(upper, low_half, high_half), bit)
        bit //= 2
    return value


def swap(value):
    return lax.ppermute(value, "tensor", [(0, 1), (1, 0)])


def spread(own):
    if lax.axis_size("tensor") == 2:
        return [own, swap(own)]
    return [lax.all_gather(own, "tensor", axis=1, tiled=True)]


def joined(parts):
    return parts[0] if len(parts) == 1 else jnp.concatenate(parts, axis=1)


def collect(parts, weight):
    def term(part):
        return jnp.einsum("lse,fe->lsf", part, weight, preferred_element_type=jnp.float32).astype(
            jnp.bfloat16
        )

    if len(parts) == 2:
        arrived = swap(term(parts[1]))
        return term(parts[0]).astype(jnp.float32) + arrived.astype(jnp.float32)
    return lax.psum_scatter(term(parts[0]), "tensor", scatter_dimension=1, tiled=True).astype(
        jnp.float32
    )


def body(
    tokens, cond, qkv_weight, out_weight, up_weight, down_weight, ada_weight, ada_bias, cotangent
):
    me = lax.axis_index("dp")
    width = tokens.shape[2]
    score_scale = HEAD_DIM ** (-0.5)
    qkv_columns, up_columns = qkv_weight.shape[1], up_weight.shape[1]
    first_weights = lax.all_gather(
        jnp.concatenate([qkv_weight, out_weight], axis=1), "dp", axis=0, tiled=True
    )
    second_weights = lax.all_gather(
        jnp.concatenate([up_weight, down_weight], axis=1), "dp", axis=0, tiled=True
    )
    w_qkv, w_out = first_weights[:, :qkv_columns], first_weights[:, qkv_columns:]
    w_up, w_down = second_weights[:, :up_columns], second_weights[:, up_columns:]
    own_tokens = tokens.transpose(1, 0, 2)
    own_cotangent = cotangent.transpose(1, 0, 2)
    token_parts = spread(own_tokens)
    cotangent_parts = spread(own_cotangent)
    cond_value = cond.astype(jnp.float32)
    cond_act = jax.nn.silu(cond_value).astype(jnp.bfloat16)
    all_cond_act = gather_small(cond_act)
    ada_rows, ada_columns = ada_weight.shape
    bias_columns = ada_bias.shape[0]
    my_cond_act = lax.dynamic_slice_in_dim(all_cond_act, me * ada_rows, ada_rows, axis=1)
    mod_term = jnp.dot(my_cond_act, ada_weight, preferred_element_type=jnp.float32)
    placed_bias = lax.dynamic_update_slice_in_dim(
        jnp.zeros((ada_columns,), jnp.float32),
        ada_bias.astype(jnp.float32),
        me * bias_columns,
        axis=0,
    )
    modulation = scatter_small(mod_term + placed_bias[None, :])
    shift1, scale1, gate1, shift2, scale2, gate2 = jnp.split(modulation[:, None, :], 6, axis=-1)
    residual = own_tokens.astype(jnp.float32)
    full_normed1 = joined(
        [
            modulate(part.astype(jnp.float32), shift1, scale1).astype(jnp.bfloat16)
            for part in token_parts
        ]
    )
    query_key_value = jnp.einsum(
        "lsd,dw->lsw", full_normed1, w_qkv, preferred_element_type=jnp.float32
    ).astype(jnp.bfloat16)
    attended, log_total = attention_forward(query_key_value, score_scale)
    own_count = residual.shape[1]
    attended_parts = (
        [attended[:, :own_count], attended[:, own_count:]] if len(token_parts) == 2 else [attended]
    )
    branch = collect(attended_parts, w_out)
    middle = residual + gate1 * branch
    normed2 = modulate(middle, shift2, scale2).astype(jnp.bfloat16)
    normed2_parts = spread(normed2)
    inner_parts = [
        jnp.einsum("lsd,dw->lsw", part, w_up, preferred_element_type=jnp.float32)
        for part in normed2_parts
    ]
    activation_parts = [gelu_tanh(part).astype(jnp.bfloat16) for part in inner_parts]
    mlp_out = collect(activation_parts, w_down)
    mixed = middle + gate2 * mlp_out
    grad_output = own_cotangent.astype(jnp.float32)
    grad_gate2 = jnp.sum(grad_output * mlp_out, axis=1)
    grad_mlp_parts = [
        (part.astype(jnp.float32) * gate2).astype(jnp.bfloat16) for part in cotangent_parts
    ]
    grad_inner_parts = []
    for grad_part, inner_part in zip(grad_mlp_parts, inner_parts):
        grad_act = jnp.einsum("lsf,fe->lse", grad_part, w_down, preferred_element_type=jnp.float32)
        grad_inner_parts.append(
            jax.vjp(gelu_tanh, inner_part)[1](grad_act)[0].astype(jnp.bfloat16)
        )
    grad_normed2 = collect(grad_inner_parts, w_up)
    grad_down = jnp.einsum(
        "lsf,lse->fe",
        joined(grad_mlp_parts),
        joined(activation_parts),
        preferred_element_type=jnp.float32,
    )
    grad_up = jnp.einsum(
        "lsd,lse->de",
        joined(normed2_parts),
        joined(grad_inner_parts),
        preferred_element_type=jnp.float32,
    )
    second_grads = jnp.concatenate(
        [grad_up.astype(jnp.bfloat16), grad_down.astype(jnp.bfloat16)], axis=1
    )
    mod_pull2 = jax.vjp(modulate, middle, shift2, scale2)[1]
    grad_middle, grad_shift2, grad_scale2 = mod_pull2(grad_normed2)
    grad_middle = grad_middle + grad_output
    grad_gate1 = jnp.sum(grad_middle * branch, axis=1)
    grad_branch = (grad_middle * gate1).astype(jnp.bfloat16)
    full_grad_branch = joined(spread(grad_branch))
    full_grad_branch, second_grads = lax.optimization_barrier((full_grad_branch, second_grads))
    second_grads = lax.psum_scatter(second_grads, "dp", scatter_dimension=0, tiled=True)
    grad_attended = jnp.einsum(
        "lsf,fe->lse", full_grad_branch, w_out, preferred_element_type=jnp.float32
    ).astype(jnp.bfloat16)
    grad_out = jnp.einsum(
        "lsf,lse->fe", full_grad_branch, attended, preferred_element_type=jnp.float32
    ).astype(jnp.bfloat16)
    grad_query_key_value = attention_backward(
        query_key_value, attended, log_total, grad_attended, score_scale
    )
    grad_qkv = jnp.einsum(
        "lsd,lsw->dw", full_normed1, grad_query_key_value, preferred_element_type=jnp.float32
    ).astype(jnp.bfloat16)
    first_grads = lax.psum_scatter(
        jnp.concatenate([grad_qkv, grad_out], axis=1), "dp", scatter_dimension=0, tiled=True
    )
    grad_parts = (
        [grad_query_key_value[:, :own_count], grad_query_key_value[:, own_count:]]
        if len(token_parts) == 2
        else [grad_query_key_value]
    )
    grad_normed1 = collect(grad_parts, w_qkv)
    mod_pull1 = jax.vjp(modulate, residual, shift1, scale1)[1]
    grad_residual, grad_shift1, grad_scale1 = mod_pull1(grad_normed1)
    grad_tokens = grad_residual + grad_middle
    mod_part = jnp.concatenate(
        [
            grad_shift1[:, 0],
            grad_scale1[:, 0],
            grad_gate1,
            grad_shift2[:, 0],
            grad_scale2[:, 0],
            grad_gate2,
        ],
        axis=-1,
    )
    if lax.axis_size("tensor") == 2:
        mod_sum = mod_part + swap(mod_part)
    else:
        mod_sum = lax.psum(mod_part, "tensor")
    all_grad_mod = gather_small(mod_sum.astype(jnp.bfloat16))
    grad_bias = jnp.sum(
        lax.dynamic_slice_in_dim(all_grad_mod, me * bias_columns, bias_columns, axis=1).astype(
            jnp.float32
        ),
        axis=0,
    )
    grad_ada = jnp.einsum(
        "ld,lk->dk", my_cond_act, all_grad_mod, preferred_element_type=jnp.float32
    )
    cond_term = jnp.einsum(
        "lk,dk->ld", all_grad_mod, ada_weight, preferred_element_type=jnp.float32
    )
    grad_cond_act = scatter_small(
        lax.dynamic_update_slice_in_dim(
            jnp.zeros((cond_term.shape[0], width), jnp.float32), cond_term, me * ada_rows, axis=1
        )
    )
    sigmoid_c = jax.nn.sigmoid(cond_value)
    grad_cond = grad_cond_act * sigmoid_c * (1.0 + cond_value * (1.0 - sigmoid_c))
    return (
        mixed.transpose(1, 0, 2),
        grad_tokens.transpose(1, 0, 2),
        grad_cond,
        first_grads[:, :qkv_columns].astype(jnp.float32),
        first_grads[:, qkv_columns:].astype(jnp.float32),
        second_grads[:, :up_columns].astype(jnp.float32),
        second_grads[:, up_columns:].astype(jnp.float32),
        grad_ada,
        grad_bias,
    )


def solution(mesh):
    return jax.shard_map(
        body,
        mesh=mesh,
        in_specs=(
            P("tensor", "dp", None),
            P("dp", None),
            P("dp", "tensor"),
            P("dp", "tensor"),
            P("dp", "tensor"),
            P("dp", "tensor"),
            P("dp", None),
            P("dp"),
            P("tensor", "dp", None),
        ),
        out_specs=(
            P("tensor", "dp", None),
            P("tensor", "dp", None),
            P("dp", None),
            P("dp", "tensor"),
            P("dp", "tensor"),
            P("dp", "tensor"),
            P("dp", "tensor"),
            P("dp", None),
            P("dp"),
        ),
        check_vma=False,
    )
```

```python
import functools

import jax
import jax.numpy as jnp
from jax import lax
from jax.experimental import pallas as pl
from jax.experimental.pallas import tpu as pltpu
from jax.sharding import PartitionSpec as P

HEAD_DIM = 64
KERNEL_VMEM = 40 * 2**20


epsilon = 1e-06


def layer_norm(inputs):
    centred = inputs - jnp.mean(inputs, axis=-1, keepdims=True)
    return centred * lax.rsqrt(jnp.mean(centred * centred, axis=-1, keepdims=True) + epsilon)


def modulate(inputs, shift_vec, scale_vec):
    return layer_norm(inputs) * (1.0 + scale_vec) + shift_vec


def gelu_tanh(inputs):
    return jax.nn.gelu(inputs, approximate=True)


def row_dot(left, right):
    return lax.dot_general(left, right, (((1,), (1,)), ((), ())), preferred_element_type=jnp.float32)


def column_dot(left, right):
    return lax.dot_general(left, right, (((0,), (0,)), ((), ())), preferred_element_type=jnp.float32)


def forward_kernel(score_scale, qkv_ref, attended_ref, log_ref):
    seq_len = qkv_ref.shape[1]
    block_rows = min(512, seq_len)
    for head in range(2):
        first = head * 3 * HEAD_DIM
        key_head = qkv_ref[0, :, first + HEAD_DIM : first + 2 * HEAD_DIM]
        value_head = qkv_ref[0, :, first + 2 * HEAD_DIM : first + 3 * HEAD_DIM]
        for start in range(0, seq_len, block_rows):
            rows = slice(start, start + block_rows)
            query_block = qkv_ref[0, rows, first : first + HEAD_DIM] * score_scale
            scores = row_dot(key_head, query_block)
            row_max = jnp.max(scores, axis=0, keepdims=True)
            shifted = jnp.exp(scores - row_max)
            denom_sum = jnp.sum(shifted, axis=0, keepdims=True)
            result = column_dot(value_head, shifted.astype(jnp.bfloat16)) / denom_sum
            attended_ref[0, rows, head * HEAD_DIM : (head + 1) * HEAD_DIM] = result.T.astype(
                jnp.bfloat16
            )
            log_ref[0, 0, head : head + 1, rows] = row_max + jnp.log(denom_sum)


def backward_kernel(score_scale, qkv_ref, grad_ref, log_ref, out_ref):
    seq_len = qkv_ref.shape[1]
    block_rows = min(512, seq_len)
    for head in range(2):
        first = head * 3 * HEAD_DIM
        key_head = qkv_ref[0, :, first + HEAD_DIM : first + 2 * HEAD_DIM]
        value_head = qkv_ref[0, :, first + 2 * HEAD_DIM : first + 3 * HEAD_DIM]
        grad_keys = jnp.zeros((seq_len, HEAD_DIM), jnp.float32)
        grad_values = jnp.zeros((seq_len, HEAD_DIM), jnp.float32)
        for start in range(0, seq_len, block_rows):
            rows = slice(start, start + block_rows)
            query_block = qkv_ref[0, rows, first : first + HEAD_DIM] * score_scale
            grad_block = grad_ref[0, rows, head * HEAD_DIM : (head + 1) * HEAD_DIM]
            scores = row_dot(key_head, query_block)
            probs = jnp.exp(scores - log_ref[0, 0, head : head + 1, rows])
            grad_probs = row_dot(value_head, grad_block)
            delta = jnp.sum(grad_probs * probs, axis=0, keepdims=True)
            grad_scores = (probs * (grad_probs - delta)).astype(jnp.bfloat16)
            grad_query = column_dot(key_head, grad_scores) * score_scale
            out_ref[0, rows, first : first + HEAD_DIM] = grad_query.T.astype(jnp.bfloat16)
            grad_keys += jnp.dot(grad_scores, query_block, preferred_element_type=jnp.float32)
            grad_values += jnp.dot(
                probs.astype(jnp.bfloat16), grad_block, preferred_element_type=jnp.float32
            )
        out_ref[0, :, first + HEAD_DIM : first + 2 * HEAD_DIM] = grad_keys.astype(jnp.bfloat16)
        out_ref[0, :, first + 2 * HEAD_DIM : first + 3 * HEAD_DIM] = grad_values.astype(
            jnp.bfloat16
        )


def head_pair_spec(seq_len, columns):
    return pl.BlockSpec((1, seq_len, columns), lambda latent, pair: (latent, 0, pair))


def log_spec(seq_len):
    return pl.BlockSpec((1, 1, 2, seq_len), lambda latent, pair: (latent, pair, 0, 0))


def attention_forward(query_key_value, score_scale):
    latents, seq_len, features = query_key_value.shape
    pairs = features // (6 * HEAD_DIM)
    work = latents * pairs * 2 * seq_len * seq_len
    return pl.pallas_call(
        functools.partial(forward_kernel, score_scale),
        grid=(latents, pairs),
        in_specs=[head_pair_spec(seq_len, 6 * HEAD_DIM)],
        out_specs=[head_pair_spec(seq_len, 2 * HEAD_DIM), log_spec(seq_len)],
        out_shape=[
            jax.ShapeDtypeStruct((latents, seq_len, features // 3), jnp.bfloat16),
            jax.ShapeDtypeStruct((latents, pairs, 2, seq_len), jnp.float32),
        ],
        compiler_params=pltpu.CompilerParams(vmem_limit_bytes=KERNEL_VMEM),
        cost_estimate=pl.CostEstimate(
            flops=4 * work * HEAD_DIM * 4, bytes_accessed=8 * latents * seq_len * features // 3, transcendentals=work
        ),
        name="attention_forward",
    )(query_key_value)


def attention_backward(query_key_value, log_total, grad_attended, score_scale):
    latents, seq_len, features = query_key_value.shape
    pairs = features // (6 * HEAD_DIM)
    work = latents * pairs * 2 * seq_len * seq_len
    return pl.pallas_call(
        functools.partial(backward_kernel, score_scale),
        grid=(latents, pairs),
        in_specs=[
            head_pair_spec(seq_len, 6 * HEAD_DIM),
            head_pair_spec(seq_len, 2 * HEAD_DIM),
            log_spec(seq_len),
        ],
        out_specs=head_pair_spec(seq_len, 6 * HEAD_DIM),
        out_shape=jax.ShapeDtypeStruct((latents, seq_len, features), jnp.bfloat16),
        compiler_params=pltpu.CompilerParams(vmem_limit_bytes=KERNEL_VMEM),
        cost_estimate=pl.CostEstimate(
            flops=10 * work * HEAD_DIM * 4, bytes_accessed=14 * latents * seq_len * features // 3, transcendentals=work
        ),
        name="attention_backward",
    )(query_key_value, grad_attended, log_total)


def dp_partner(value, bit):
    size = lax.axis_size("dp")
    return lax.ppermute(value, "dp", [(index, index ^ bit) for index in range(size)])


def gather_small(value):
    size, me, bit = lax.axis_size("dp"), lax.axis_index("dp"), 1
    while bit < size:
        other = dp_partner(value, bit)
        upper = (me & bit) != 0
        value = jnp.concatenate([jnp.where(upper, other, value), jnp.where(upper, value, other)], axis=0)
        bit *= 2
    return value


def scatter_small(value):
    me, bit = lax.axis_index("dp"), lax.axis_size("dp") // 2
    while bit >= 1:
        half = value.shape[0] // 2
        upper = (me & bit) != 0
        low_half, high_half = value[:half], value[half:]
        kept = jnp.where(upper, high_half, low_half)
        value = kept + dp_partner(jnp.where(upper, low_half, high_half), bit)
        bit //= 2
    return value


def swap(value):
    return lax.ppermute(value, "tensor", [(0, 1), (1, 0)])


def spread(own):
    if lax.axis_size("tensor") == 2:
        return [own, swap(own)]
    return [lax.all_gather(own, "tensor", axis=1, tiled=True)]


def joined(parts):
    return parts[0] if len(parts) == 1 else jnp.concatenate(parts, axis=1)


def collect(parts, weight):
    def term(part):
        return jnp.einsum("lse,fe->lsf", part, weight, preferred_element_type=jnp.float32).astype(
            jnp.bfloat16
        )

    if len(parts) == 2:
        arrived = swap(term(parts[1]))
        return term(parts[0]).astype(jnp.float32) + arrived.astype(jnp.float32)
    return lax.psum_scatter(term(parts[0]), "tensor", scatter_dimension=1, tiled=True).astype(
        jnp.float32
    )


def body(
    tokens, cond, qkv_weight, out_weight, up_weight, down_weight, ada_weight, ada_bias, cotangent
):
    me = lax.axis_index("dp")
    width = tokens.shape[2]
    score_scale = HEAD_DIM ** (-0.5)
    qkv_columns, up_columns = qkv_weight.shape[1], up_weight.shape[1]
    first_weights = lax.all_gather(
        jnp.concatenate([qkv_weight, out_weight], axis=1), "dp", axis=0, tiled=True
    )
    second_weights = lax.all_gather(
        jnp.concatenate([up_weight, down_weight], axis=1), "dp", axis=0, tiled=True
    )
    w_qkv, w_out = first_weights[:, :qkv_columns], first_weights[:, qkv_columns:]
    w_up, w_down = second_weights[:, :up_columns], second_weights[:, up_columns:]
    own_tokens = tokens.transpose(1, 0, 2)
    own_cotangent = cotangent.transpose(1, 0, 2)
    token_parts = spread(own_tokens)
    cotangent_parts = spread(own_cotangent)
    token_parts, cotangent_parts = lax.optimization_barrier((token_parts, cotangent_parts))
    cond_value = cond.astype(jnp.float32)
    cond_act = jax.nn.silu(cond_value).astype(jnp.bfloat16)
    all_cond_act = gather_small(cond_act)
    ada_rows, ada_columns = ada_weight.shape
    bias_columns = ada_bias.shape[0]
    my_cond_act = lax.dynamic_slice_in_dim(all_cond_act, me * ada_rows, ada_rows, axis=1)
    mod_term = jnp.dot(my_cond_act, ada_weight, preferred_element_type=jnp.float32)
    placed_bias = lax.dynamic_update_slice_in_dim(
        jnp.zeros((ada_columns,), jnp.float32),
        ada_bias.astype(jnp.float32),
        me * bias_columns,
        axis=0,
    )
    modulation = scatter_small(mod_term + placed_bias[None, :])
    shift1, scale1, gate1, shift2, scale2, gate2 = jnp.split(modulation[:, None, :], 6, axis=-1)
    residual = own_tokens.astype(jnp.float32)
    full_normed1 = joined(
        [
            modulate(part.astype(jnp.float32), shift1, scale1).astype(jnp.bfloat16)
            for part in token_parts
        ]
    )
    query_key_value = jnp.einsum(
        "lsd,dw->lsw", full_normed1, w_qkv, preferred_element_type=jnp.float32
    ).astype(jnp.bfloat16)
    attended, log_total = attention_forward(query_key_value, score_scale)
    own_count = residual.shape[1]
    attended_parts = (
        [attended[:, :own_count], attended[:, own_count:]] if len(token_parts) == 2 else [attended]
    )
    branch = collect(attended_parts, w_out)
    middle = residual + gate1 * branch
    normed2 = modulate(middle, shift2, scale2).astype(jnp.bfloat16)
    normed2_parts = spread(normed2)
    inner_parts = [
        jnp.einsum("lsd,dw->lsw", part, w_up, preferred_element_type=jnp.float32)
        for part in normed2_parts
    ]
    activation_parts = [gelu_tanh(part).astype(jnp.bfloat16) for part in inner_parts]
    mlp_out = collect(activation_parts, w_down)
    mixed = middle + gate2 * mlp_out
    grad_output = own_cotangent.astype(jnp.float32)
    grad_gate2 = jnp.sum(grad_output * mlp_out, axis=1)
    grad_mlp_parts = [
        (part.astype(jnp.float32) * gate2).astype(jnp.bfloat16) for part in cotangent_parts
    ]
    grad_inner_parts = []
    for grad_part, inner_part in zip(grad_mlp_parts, inner_parts):
        grad_act = jnp.einsum("lsf,fe->lse", grad_part, w_down, preferred_element_type=jnp.float32)
        grad_inner_parts.append(
            jax.vjp(gelu_tanh, inner_part)[1](grad_act)[0].astype(jnp.bfloat16)
        )
    grad_normed2 = collect(grad_inner_parts, w_up)
    grad_down = jnp.einsum(
        "lsf,lse->fe",
        joined(grad_mlp_parts),
        joined(activation_parts),
        preferred_element_type=jnp.float32,
    )
    grad_up = jnp.einsum(
        "lsd,lse->de",
        joined(normed2_parts),
        joined(grad_inner_parts),
        preferred_element_type=jnp.float32,
    )
    second_grads = jnp.concatenate(
        [grad_up.astype(jnp.bfloat16), grad_down.astype(jnp.bfloat16)], axis=1
    )
    mod_pull2 = jax.vjp(modulate, middle, shift2, scale2)[1]
    grad_middle, grad_shift2, grad_scale2 = mod_pull2(grad_normed2)
    grad_middle = grad_middle + grad_output
    grad_gate1 = jnp.sum(grad_middle * branch, axis=1)
    grad_branch = (grad_middle * gate1).astype(jnp.bfloat16)
    full_grad_branch = joined(spread(grad_branch))
    full_grad_branch, second_grads = lax.optimization_barrier((full_grad_branch, second_grads))
    second_grads = lax.psum_scatter(second_grads, "dp", scatter_dimension=0, tiled=True)
    grad_attended = jnp.einsum(
        "lsf,fe->lse", full_grad_branch, w_out, preferred_element_type=jnp.float32
    ).astype(jnp.bfloat16)
    grad_out = jnp.einsum(
        "lsf,lse->fe", full_grad_branch, attended, preferred_element_type=jnp.float32
    ).astype(jnp.bfloat16)
    grad_query_key_value = attention_backward(
        query_key_value, log_total, grad_attended, score_scale
    )
    grad_qkv = jnp.einsum(
        "lsd,lsw->dw", full_normed1, grad_query_key_value, preferred_element_type=jnp.float32
    ).astype(jnp.bfloat16)
    first_grads, second_grads = lax.optimization_barrier(
        (jnp.concatenate([grad_qkv, grad_out], axis=1), second_grads)
    )
    first_grads = lax.psum_scatter(first_grads, "dp", scatter_dimension=0, tiled=True)
    grad_parts = (
        [grad_query_key_value[:, :own_count], grad_query_key_value[:, own_count:]]
        if len(token_parts) == 2
        else [grad_query_key_value]
    )
    grad_normed1 = collect(grad_parts, w_qkv)
    mod_pull1 = jax.vjp(modulate, residual, shift1, scale1)[1]
    grad_residual, grad_shift1, grad_scale1 = mod_pull1(grad_normed1)
    grad_tokens = grad_residual + grad_middle
    mod_part = jnp.concatenate(
        [
            grad_shift1[:, 0],
            grad_scale1[:, 0],
            grad_gate1,
            grad_shift2[:, 0],
            grad_scale2[:, 0],
            grad_gate2,
        ],
        axis=-1,
    )
    if lax.axis_size("tensor") == 2:
        mod_sum = mod_part + swap(mod_part)
    else:
        mod_sum = lax.psum(mod_part, "tensor")
    all_grad_mod = gather_small(mod_sum.astype(jnp.bfloat16))
    grad_bias = jnp.sum(
        lax.dynamic_slice_in_dim(all_grad_mod, me * bias_columns, bias_columns, axis=1).astype(
            jnp.float32
        ),
        axis=0,
    )
    grad_ada = jnp.einsum(
        "ld,lk->dk", my_cond_act, all_grad_mod, preferred_element_type=jnp.float32
    )
    cond_term = jnp.einsum(
        "lk,dk->ld", all_grad_mod, ada_weight, preferred_element_type=jnp.float32
    )
    grad_cond_act = scatter_small(
        lax.dynamic_update_slice_in_dim(
            jnp.zeros((cond_term.shape[0], width), jnp.float32), cond_term, me * ada_rows, axis=1
        )
    )
    sigmoid_c = jax.nn.sigmoid(cond_value)
    grad_cond = grad_cond_act * sigmoid_c * (1.0 + cond_value * (1.0 - sigmoid_c))
    return (
        mixed.transpose(1, 0, 2),
        grad_tokens.transpose(1, 0, 2),
        grad_cond,
        first_grads[:, :qkv_columns].astype(jnp.float32),
        first_grads[:, qkv_columns:].astype(jnp.float32),
        second_grads[:, :up_columns].astype(jnp.float32),
        second_grads[:, up_columns:].astype(jnp.float32),
        grad_ada,
        grad_bias,
    )


def solution(mesh):
    return jax.shard_map(
        body,
        mesh=mesh,
        in_specs=(
            P("tensor", "dp", None),
            P("dp", None),
            P("dp", "tensor"),
            P("dp", "tensor"),
            P("dp", "tensor"),
            P("dp", "tensor"),
            P("dp", None),
            P("dp"),
            P("tensor", "dp", None),
        ),
        out_specs=(
            P("tensor", "dp", None),
            P("tensor", "dp", None),
            P("dp", None),
            P("dp", "tensor"),
            P("dp", "tensor"),
            P("dp", "tensor"),
            P("dp", "tensor"),
            P("dp", None),
            P("dp"),
        ),
        check_vma=False,
    )
```

```python
import functools

import jax
import jax.numpy as jnp
from jax import lax
from jax.experimental import pallas as pl
from jax.experimental.pallas import tpu as pltpu
from jax.sharding import PartitionSpec as P

HEAD_DIM = 64
KERNEL_VMEM = 40 * 2**20


epsilon = 1e-06


def layer_norm(inputs):
    centred = inputs - jnp.mean(inputs, axis=-1, keepdims=True)
    return centred * lax.rsqrt(jnp.mean(centred * centred, axis=-1, keepdims=True) + epsilon)


def modulate(inputs, shift_vec, scale_vec):
    return layer_norm(inputs) * (1.0 + scale_vec) + shift_vec


def gelu_tanh(inputs):
    return jax.nn.gelu(inputs, approximate=True)


def row_dot(left, right):
    return lax.dot_general(left, right, (((1,), (1,)), ((), ())), preferred_element_type=jnp.float32)


def column_dot(left, right):
    return lax.dot_general(left, right, (((0,), (0,)), ((), ())), preferred_element_type=jnp.float32)


def forward_kernel(score_scale, qkv_ref, attended_ref, log_ref):
    seq_len = qkv_ref.shape[1]
    block_rows = min(512, seq_len)
    for head in range(2):
        first = head * 3 * HEAD_DIM
        key_head = qkv_ref[0, :, first + HEAD_DIM : first + 2 * HEAD_DIM]
        value_head = qkv_ref[0, :, first + 2 * HEAD_DIM : first + 3 * HEAD_DIM]
        for start in range(0, seq_len, block_rows):
            rows = slice(start, start + block_rows)
            query_block = qkv_ref[0, rows, first : first + HEAD_DIM] * score_scale
            scores = row_dot(key_head, query_block)
            row_max = jnp.max(scores, axis=0, keepdims=True)
            shifted = jnp.exp(scores - row_max)
            denom_sum = jnp.sum(shifted, axis=0, keepdims=True)
            result = column_dot(value_head, shifted.astype(jnp.bfloat16)) / denom_sum
            attended_ref[0, rows, head * HEAD_DIM : (head + 1) * HEAD_DIM] = result.T.astype(
                jnp.bfloat16
            )
            log_ref[0, 0, head : head + 1, rows] = row_max + jnp.log(denom_sum)


def backward_kernel(score_scale, qkv_ref, grad_ref, log_ref, out_ref):
    seq_len = qkv_ref.shape[1]
    block_rows = min(512, seq_len)
    for head in range(2):
        first = head * 3 * HEAD_DIM
        key_head = qkv_ref[0, :, first + HEAD_DIM : first + 2 * HEAD_DIM]
        value_head = qkv_ref[0, :, first + 2 * HEAD_DIM : first + 3 * HEAD_DIM]
        grad_keys = jnp.zeros((seq_len, HEAD_DIM), jnp.float32)
        grad_values = jnp.zeros((seq_len, HEAD_DIM), jnp.float32)
        for start in range(0, seq_len, block_rows):
            rows = slice(start, start + block_rows)
            query_block = qkv_ref[0, rows, first : first + HEAD_DIM] * score_scale
            grad_block = grad_ref[0, rows, head * HEAD_DIM : (head + 1) * HEAD_DIM]
            scores = row_dot(key_head, query_block)
            probs = jnp.exp(scores - log_ref[0, 0, head : head + 1, rows])
            grad_probs = row_dot(value_head, grad_block)
            delta = jnp.sum(grad_probs * probs, axis=0, keepdims=True)
            grad_scores = (probs * (grad_probs - delta)).astype(jnp.bfloat16)
            grad_query = column_dot(key_head, grad_scores) * score_scale
            out_ref[0, rows, first : first + HEAD_DIM] = grad_query.T.astype(jnp.bfloat16)
            grad_keys += jnp.dot(grad_scores, query_block, preferred_element_type=jnp.float32)
            grad_values += jnp.dot(
                probs.astype(jnp.bfloat16), grad_block, preferred_element_type=jnp.float32
            )
        out_ref[0, :, first + HEAD_DIM : first + 2 * HEAD_DIM] = grad_keys.astype(jnp.bfloat16)
        out_ref[0, :, first + 2 * HEAD_DIM : first + 3 * HEAD_DIM] = grad_values.astype(
            jnp.bfloat16
        )


def head_pair_spec(seq_len, columns):
    return pl.BlockSpec((1, seq_len, columns), lambda latent, pair: (latent, 0, pair))


def log_spec(seq_len):
    return pl.BlockSpec((1, 1, 2, seq_len), lambda latent, pair: (latent, pair, 0, 0))


def attention_forward(query_key_value, score_scale):
    latents, seq_len, features = query_key_value.shape
    pairs = features // (6 * HEAD_DIM)
    work = latents * pairs * 2 * seq_len * seq_len
    return pl.pallas_call(
        functools.partial(forward_kernel, score_scale),
        grid=(latents, pairs),
        in_specs=[head_pair_spec(seq_len, 6 * HEAD_DIM)],
        out_specs=[head_pair_spec(seq_len, 2 * HEAD_DIM), log_spec(seq_len)],
        out_shape=[
            jax.ShapeDtypeStruct((latents, seq_len, features // 3), jnp.bfloat16),
            jax.ShapeDtypeStruct((latents, pairs, 2, seq_len), jnp.float32),
        ],
        compiler_params=pltpu.CompilerParams(vmem_limit_bytes=KERNEL_VMEM),
        cost_estimate=pl.CostEstimate(
            flops=4 * work * HEAD_DIM * 4, bytes_accessed=8 * latents * seq_len * features // 3, transcendentals=work
        ),
        name="attention_forward",
    )(query_key_value)


def attention_backward(query_key_value, log_total, grad_attended, score_scale):
    latents, seq_len, features = query_key_value.shape
    pairs = features // (6 * HEAD_DIM)
    work = latents * pairs * 2 * seq_len * seq_len
    return pl.pallas_call(
        functools.partial(backward_kernel, score_scale),
        grid=(latents, pairs),
        in_specs=[
            head_pair_spec(seq_len, 6 * HEAD_DIM),
            head_pair_spec(seq_len, 2 * HEAD_DIM),
            log_spec(seq_len),
        ],
        out_specs=head_pair_spec(seq_len, 6 * HEAD_DIM),
        out_shape=jax.ShapeDtypeStruct((latents, seq_len, features), jnp.bfloat16),
        compiler_params=pltpu.CompilerParams(vmem_limit_bytes=KERNEL_VMEM),
        cost_estimate=pl.CostEstimate(
            flops=10 * work * HEAD_DIM * 4, bytes_accessed=14 * latents * seq_len * features // 3, transcendentals=work
        ),
        name="attention_backward",
    )(query_key_value, grad_attended, log_total)


def dp_partner(value, bit):
    size = lax.axis_size("dp")
    return lax.ppermute(value, "dp", [(index, index ^ bit) for index in range(size)])


def gather_small(value):
    size, me, bit = lax.axis_size("dp"), lax.axis_index("dp"), 1
    while bit < size:
        other = dp_partner(value, bit)
        upper = (me & bit) != 0
        value = jnp.concatenate([jnp.where(upper, other, value), jnp.where(upper, value, other)], axis=0)
        bit *= 2
    return value


def scatter_step(value, bit):
    half = value.shape[0] // 2
    upper = (lax.axis_index("dp") & bit) != 0
    low_half, high_half = value[:half], value[half:]
    kept = jnp.where(upper, high_half, low_half)
    return kept + dp_partner(jnp.where(upper, low_half, high_half), bit)


def scatter_small(value, bit):
    while bit >= 1:
        value = scatter_step(value, bit)
        bit //= 2
    return value


def scatter_matrix(value, bit_order):
    me, size, columns = lax.axis_index("dp"), lax.axis_size("dp"), value.shape[1]
    rows = value.shape[0] // size
    left = list(range(size.bit_length() - 2, -1, -1))
    value = value.reshape((2,) * len(left) + (rows, columns))
    for place in bit_order:
        axis, bit = left.index(place), 1 << place
        upper = (me & bit) != 0
        low_half = lax.index_in_dim(value, 0, axis, keepdims=False)
        high_half = lax.index_in_dim(value, 1, axis, keepdims=False)
        arrived = dp_partner(jnp.where(upper, low_half, high_half), bit)
        kept = jnp.where(upper, high_half, low_half)
        value = (kept.astype(jnp.float32) + arrived.astype(jnp.float32)).astype(jnp.bfloat16)
        left.pop(axis)
    return value


def swap(value):
    return lax.ppermute(value, "tensor", [(0, 1), (1, 0)])


def spread(own):
    if lax.axis_size("tensor") == 2:
        return [own, swap(own)]
    return [lax.all_gather(own, "tensor", axis=1, tiled=True)]


def joined(parts):
    return parts[0] if len(parts) == 1 else jnp.concatenate(parts, axis=1)


def collect(parts, weight):
    def term(part):
        return jnp.einsum("lse,fe->lsf", part, weight, preferred_element_type=jnp.float32).astype(
            jnp.bfloat16
        )

    if len(parts) == 2:
        arrived = swap(term(parts[1]))
        return term(parts[0]).astype(jnp.float32) + arrived.astype(jnp.float32)
    return lax.psum_scatter(term(parts[0]), "tensor", scatter_dimension=1, tiled=True).astype(
        jnp.float32
    )


def body(
    tokens, cond, qkv_weight, out_weight, up_weight, down_weight, ada_weight, ada_bias, cotangent
):
    me = lax.axis_index("dp")
    width = tokens.shape[2]
    score_scale = HEAD_DIM ** (-0.5)
    qkv_columns, up_columns = qkv_weight.shape[1], up_weight.shape[1]
    first_weights = lax.all_gather(
        jnp.concatenate([qkv_weight, out_weight], axis=1), "dp", axis=0, tiled=True
    )
    second_weights = lax.all_gather(
        jnp.concatenate([up_weight, down_weight], axis=1), "dp", axis=0, tiled=True
    )
    w_qkv, w_out = first_weights[:, :qkv_columns], first_weights[:, qkv_columns:]
    w_up, w_down = second_weights[:, :up_columns], second_weights[:, up_columns:]
    own_tokens = tokens.transpose(1, 0, 2)
    own_cotangent = cotangent.transpose(1, 0, 2)
    token_parts = spread(own_tokens)
    cotangent_parts = spread(own_cotangent)
    cond_value = cond.astype(jnp.float32)
    cond_act = jax.nn.silu(cond_value).astype(jnp.bfloat16)
    all_cond_act, token_parts = lax.optimization_barrier((gather_small(cond_act), token_parts))
    ada_rows, ada_columns = ada_weight.shape
    bias_columns = ada_bias.shape[0]
    my_cond_act = lax.dynamic_slice_in_dim(all_cond_act, me * ada_rows, ada_rows, axis=1)
    mod_term = jnp.dot(my_cond_act, ada_weight, preferred_element_type=jnp.float32)
    placed_bias = lax.dynamic_update_slice_in_dim(
        jnp.zeros((ada_columns,), jnp.float32),
        ada_bias.astype(jnp.float32),
        me * bias_columns,
        axis=0,
    )
    mod_term, cotangent_parts = lax.optimization_barrier(
        (scatter_step(mod_term + placed_bias[None, :], lax.axis_size("dp") // 2), cotangent_parts)
    )
    modulation = scatter_small(mod_term, lax.axis_size("dp") // 4)
    shift1, scale1, gate1, shift2, scale2, gate2 = jnp.split(modulation[:, None, :], 6, axis=-1)
    residual = own_tokens.astype(jnp.float32)
    full_normed1 = joined(
        [
            modulate(part.astype(jnp.float32), shift1, scale1).astype(jnp.bfloat16)
            for part in token_parts
        ]
    )
    query_key_value = jnp.einsum(
        "lsd,dw->lsw", full_normed1, w_qkv, preferred_element_type=jnp.float32
    ).astype(jnp.bfloat16)
    attended, log_total = attention_forward(query_key_value, score_scale)
    own_count = residual.shape[1]
    attended_parts = (
        [attended[:, :own_count], attended[:, own_count:]] if len(token_parts) == 2 else [attended]
    )
    branch = collect(attended_parts, w_out)
    middle = residual + gate1 * branch
    normed2 = modulate(middle, shift2, scale2).astype(jnp.bfloat16)
    normed2_parts = spread(normed2)
    inner_parts = [
        jnp.einsum("lsd,dw->lsw", part, w_up, preferred_element_type=jnp.float32)
        for part in normed2_parts
    ]
    activation_parts = [gelu_tanh(part).astype(jnp.bfloat16) for part in inner_parts]
    mlp_out = collect(activation_parts, w_down)
    mixed = middle + gate2 * mlp_out
    grad_output = own_cotangent.astype(jnp.float32)
    grad_gate2 = jnp.sum(grad_output * mlp_out, axis=1)
    grad_mlp_parts = [
        (part.astype(jnp.float32) * gate2).astype(jnp.bfloat16) for part in cotangent_parts
    ]
    grad_inner_parts = []
    for grad_part, inner_part in zip(grad_mlp_parts, inner_parts):
        grad_act = jnp.einsum("lsf,fe->lse", grad_part, w_down, preferred_element_type=jnp.float32)
        grad_inner_parts.append(
            jax.vjp(gelu_tanh, inner_part)[1](grad_act)[0].astype(jnp.bfloat16)
        )
    grad_down = jnp.einsum(
        "lsf,lse->fe",
        joined(grad_mlp_parts),
        joined(activation_parts),
        preferred_element_type=jnp.float32,
    )
    grad_up = jnp.einsum(
        "lsd,lse->de",
        joined(normed2_parts),
        joined(grad_inner_parts),
        preferred_element_type=jnp.float32,
    )
    second_grads = jnp.concatenate(
        [grad_up.astype(jnp.bfloat16), grad_down.astype(jnp.bfloat16)], axis=1
    )
    grad_inner_parts, second_grads = lax.optimization_barrier((grad_inner_parts, second_grads))
    second_grads = lax.psum_scatter(second_grads, "dp", scatter_dimension=0, tiled=True)
    grad_normed2 = collect(grad_inner_parts, w_up)
    mod_pull2 = jax.vjp(modulate, middle, shift2, scale2)[1]
    grad_middle, grad_shift2, grad_scale2 = mod_pull2(grad_normed2)
    grad_middle = grad_middle + grad_output
    grad_gate1 = jnp.sum(grad_middle * branch, axis=1)
    grad_branch = (grad_middle * gate1).astype(jnp.bfloat16)
    full_grad_branch = joined(spread(grad_branch))
    grad_attended = jnp.einsum(
        "lsf,fe->lse", full_grad_branch, w_out, preferred_element_type=jnp.float32
    ).astype(jnp.bfloat16)
    grad_out = jnp.einsum(
        "lsf,lse->fe", full_grad_branch, attended, preferred_element_type=jnp.float32
    ).astype(jnp.bfloat16)
    grad_query_key_value = attention_backward(
        query_key_value, log_total, grad_attended, score_scale
    )
    grad_qkv = jnp.einsum(
        "lsd,lsw->dw", full_normed1, grad_query_key_value, preferred_element_type=jnp.float32
    ).astype(jnp.bfloat16)
    places = list(range(lax.axis_size("dp").bit_length() - 1))
    orders = (places, places[:1] + places[2:] + places[1:2])
    half_columns = qkv_columns // 2
    grad_out = scatter_matrix(grad_out, orders[0])
    grad_qkv = jnp.concatenate(
        [
            scatter_matrix(grad_qkv[:, :half_columns], orders[0]),
            scatter_matrix(grad_qkv[:, half_columns:], orders[1]),
        ],
        axis=1,
    )
    grad_parts = (
        [grad_query_key_value[:, :own_count], grad_query_key_value[:, own_count:]]
        if len(token_parts) == 2
        else [grad_query_key_value]
    )
    grad_normed1 = collect(grad_parts, w_qkv)
    mod_pull1 = jax.vjp(modulate, residual, shift1, scale1)[1]
    grad_residual, grad_shift1, grad_scale1 = mod_pull1(grad_normed1)
    grad_tokens = grad_residual + grad_middle
    mod_part = jnp.concatenate(
        [
            grad_shift1[:, 0],
            grad_scale1[:, 0],
            grad_gate1,
            grad_shift2[:, 0],
            grad_scale2[:, 0],
            grad_gate2,
        ],
        axis=-1,
    )
    if lax.axis_size("tensor") == 2:
        mod_sum = mod_part + swap(mod_part)
    else:
        mod_sum = lax.psum(mod_part, "tensor")
    all_grad_mod = gather_small(mod_sum.astype(jnp.bfloat16))
    grad_bias = jnp.sum(
        lax.dynamic_slice_in_dim(all_grad_mod, me * bias_columns, bias_columns, axis=1).astype(
            jnp.float32
        ),
        axis=0,
    )
    grad_ada = jnp.einsum(
        "ld,lk->dk", my_cond_act, all_grad_mod, preferred_element_type=jnp.float32
    )
    cond_term = jnp.einsum(
        "lk,dk->ld", all_grad_mod, ada_weight, preferred_element_type=jnp.float32
    )
    grad_cond_act = scatter_small(
        lax.dynamic_update_slice_in_dim(
            jnp.zeros((cond_term.shape[0], width), jnp.float32), cond_term, me * ada_rows, axis=1
        ),
        lax.axis_size("dp") // 2,
    )
    sigmoid_c = jax.nn.sigmoid(cond_value)
    grad_cond = grad_cond_act * sigmoid_c * (1.0 + cond_value * (1.0 - sigmoid_c))
    return (
        mixed.transpose(1, 0, 2),
        grad_tokens.transpose(1, 0, 2),
        grad_cond,
        grad_qkv.astype(jnp.float32),
        grad_out.astype(jnp.float32),
        second_grads[:, :up_columns].astype(jnp.float32),
        second_grads[:, up_columns:].astype(jnp.float32),
        grad_ada,
        grad_bias,
    )


def solution(mesh):
    return jax.shard_map(
        body,
        mesh=mesh,
        in_specs=(
            P("tensor", "dp", None),
            P("dp", None),
            P("dp", "tensor"),
            P("dp", "tensor"),
            P("dp", "tensor"),
            P("dp", "tensor"),
            P("dp", None),
            P("dp"),
            P("tensor", "dp", None),
        ),
        out_specs=(
            P("tensor", "dp", None),
            P("tensor", "dp", None),
            P("dp", None),
            P("dp", "tensor"),
            P("dp", "tensor"),
            P("dp", "tensor"),
            P("dp", "tensor"),
            P("dp", None),
            P("dp"),
        ),
        check_vma=False,
    )
```
